256 devices in a mesh: outer: 16 (over x_lo, z), inner: 16 (over y, x_hi, core).
Axes of the slice: x: 4 (x_hi: 2, x_lo: 2; x = x_hi * 2 + x_lo), y: 4, z: 8, core: 2. Of those that a mesh axis runs over, the one named last changes fastest.
Arguments:
- images: float32 [131072, 1152], P(('outer', 'inner')), may hold values from -0.5 to 0.5
- texts: float32 [131072, 1152], P(('outer', 'inner')), may hold values from -0.5 to 0.5
- partner: int32 [256, 512], P(('outer', 'inner')), may hold values from 0 to 511, each once within a row
- logit_scale: float32 [1], replicated, may hold values from 8 to 12
- logit_bias: float32 [1], replicated, may hold values from -8 to -6
Outputs:
- image_grad: float32 [131072, 1152], P(('outer', 'inner'))
- text_grad: float32 [131072, 1152], P(('outer', 'inner'))
The draws below stay inside these ranges and needn't reach their ends.
Inputs may be any that keep to these rules, and one draw needn't show every extreme that they name: Each row of partner is a permutation of the 512 rows of its block: every image pairs with exactly one text of its own block and every text with exactly one image.
All inputs are finite; a program needn't handle non-finite values.
Results may differ from the reference program's by a relative error of at most 0.00011.
Values sent between devices are 32-bit elements; how exact they have to be, the bound alone decides.
No kernel may reach another device: no remote copies, remote signals or barrier semaphores. Data moves between devices by JAX's collectives and lax.ppermute only.
A program may use at most 64 MiB of HBM per device.

```python
import math
import jax
import jax.numpy as jnp
from jax import lax

D = 1152
ROWS = 512
INNER_SPAN = 2
OUTER_SPAN = 2
BLOCKS = 256
BATCH = 131072
N_OUTER = 16
N_INNER = 16


def steps_of(own_key, dims, pieces, low, top_value):
    gain, own = 1.0, jax.random.fold_in(own_key, 6)
    for dim, blocks in pieces:
        steps = jnp.exp(jax.random.uniform(jax.random.fold_in(own, dim), (blocks,), jnp.float32, low / len(pieces), top_value / len(pieces)))
        gain = gain * jnp.repeat(steps, dims[dim] // blocks).reshape([-1 if axis == dim else 1 for axis in range(len(dims))])
    return gain


def gaussian(key, shape, scale, bound, cuts=(), kind=jnp.bfloat16):
    level = steps_of(key, shape, cuts, -0.22, 0.18) if cuts else 1.0
    drawn = jax.random.normal(key, shape, jnp.float32) * scale * level
    return jnp.minimum(jnp.maximum(drawn, -bound), bound).astype(kind)


def setup_inputs(seed: int = 0) -> dict:
    splits = jax.random.split(jax.random.key(seed), 6)
    images = gaussian(splits[0], (BATCH, D), (0.45 * D ** -0.25), 0.5, ((0, 256),), jnp.float32)
    texts = gaussian(splits[1], (BATCH, D), (0.45 * D ** -0.25), 0.5, ((0, 256),), jnp.float32)
    partner = jax.vmap(lambda own: jax.random.permutation(own, ROWS))(jax.random.split(splits[2], BLOCKS)).reshape((BLOCKS, ROWS)).astype(jnp.int32)
    logit_scale = jnp.clip(jnp.exp(jax.random.uniform(splits[3], (1,), jnp.float32, math.log(8.0), math.log(12.0))), 8.0, 12.0)
    logit_bias = jnp.clip(jax.random.uniform(splits[4], (1,), jnp.float32, -8.0, -6.0), -8.0, -6.0)
    return {"images": images, "texts": texts, "partner": partner, "logit_scale": logit_scale, "logit_bias": logit_bias}


def reference(images, texts, partner, logit_scale, logit_bias):
    scale_now = logit_scale[0]
    bias_now = logit_bias[0]
    image_blocks = images.reshape(N_OUTER, N_INNER, ROWS, D)
    text_blocks = texts.reshape(N_OUTER, N_INNER, ROWS, D)
    positive = (partner[:, :, None] == jnp.arange(ROWS, dtype=jnp.int32)[None, None, :]).astype(jnp.float32)
    positive = positive.reshape(N_OUTER, N_INNER, ROWS, ROWS)
    image_sums = jnp.zeros_like(image_blocks)
    text_sums = jnp.zeros_like(text_blocks)
    for outer_step in range(OUTER_SPAN):
        for inner_step in range(INNER_SPAN):
            paired = jnp.roll(jnp.roll(text_blocks, -outer_step, axis=0), -inner_step, axis=1)
            logits = scale_now * jnp.einsum("oird,oisd->oirs", image_blocks, paired, precision=lax.Precision.HIGHEST) + bias_now
            weight = jax.nn.sigmoid(logits)
            if outer_step == 0 and inner_step == 0:
                weight = weight - positive
            image_sums = image_sums + scale_now * jnp.einsum("oirs,oisd->oird", weight, paired, precision=lax.Precision.HIGHEST)
            share_term = scale_now * jnp.einsum("oirs,oird->oisd", weight, image_blocks, precision=lax.Precision.HIGHEST)
            text_sums = text_sums + jnp.roll(jnp.roll(share_term, outer_step, axis=0), inner_step, axis=1)
    return image_sums.reshape(BATCH, D), text_sums.reshape(BATCH, D)
```

```python
import jax
import jax.numpy as jnp
from jax import lax
from jax.experimental import pallas as pl
from jax.experimental.pallas import tpu as pltpu
from jax.sharding import PartitionSpec as P

REST = 4
TILE = 256
F32, BF16 = jnp.float32, jnp.bfloat16
ROW_ROW = (((1,), (1,)), ((), ()))
ROW_COL = (((1,), (0,)), ((), ()))
COL_COL = (((0,), (0,)), ((), ()))
VMEM = pl.BlockSpec(memory_space=pltpu.VMEM)
SMEM = pl.BlockSpec(memory_space=pltpu.SMEM)


def split(x):
    high = x.astype(BF16)
    return high, (x - high.astype(F32)).astype(BF16)


def mm(a, b, dims):
    def one(p, q):
        return lax.dot_general(p, q, dims, preferred_element_type=F32)

    return one(a[0], b[0]) + (one(a[0], b[1]) + one(a[1], b[0]))


def weights(image, text, scale, bias):
    logits = scale * mm(image, text, ROW_ROW) + bias
    return scale * jax.nn.sigmoid(logits)


def split_rows(src, high, low):
    def body(k, carry):
        rows = pl.ds(k * 128, 128)
        high[rows, :], low[rows, :] = split(src[rows, :])
        return carry

    lax.fori_loop(0, src.shape[0] // 128, body, 0)


def own_kernel(scale_ref, bias_ref, images, texts, partner, image_grad, text_grad, ih, il, th, tl):
    scale, bias = scale_ref[0], bias_ref[0]
    split_rows(texts, th, tl)
    split_rows(images, ih, il)
    text = (th[...], tl[...])
    for k in range(images.shape[0] // TILE):
        rows = pl.ds(k * TILE, TILE)
        image = (ih[rows, :], il[rows, :])
        w = weights(image, text, scale, bias)
        columns = lax.broadcasted_iota(jnp.int32, w.shape, 1)
        w = split(w - jnp.where(partner[rows, :] == columns, scale, 0.0))
        image_grad[rows, :] = mm(w, text, ROW_COL)
        term = mm(w, image, COL_COL)
        text_grad[...] = term if k == 0 else text_grad[...] + term


def piece_body(scale, bias, piece, th, tl, nh, nl, back, next_sum, ph, pq, wh, wl, next_in):
    image = split(piece[...])
    ph[...], pq[...] = image
    text = (nh[...], nl[...])
    w = split(weights(image, text, scale, bias))
    term = mm(w, image, COL_COL)
    next_sum[...] = term if next_in is None else next_in[...] + term
    total = mm(w, text, ROW_COL)
    text = (th[...], tl[...])
    w = split(weights(image, text, scale, bias))
    wh[...], wl[...] = w
    back[...] = total + mm(w, text, ROW_COL)


def first_kernel(scale_ref, bias_ref, piece, th, tl, text_next, back, next_sum, ph, pq, wh, wl, nh, nl):
    split_rows(text_next, nh, nl)
    piece_body(scale_ref[0], bias_ref[0], piece, th, tl, nh, nl, back, next_sum, ph, pq, wh, wl, None)


def next_kernel(scale_ref, bias_ref, ih, il, nh, nl, grad_in, next_in, image_grad, next_sum):
    scale, bias = scale_ref[0], bias_ref[0]
    text = (nh[...], nl[...])
    for k in range(ih.shape[0] // TILE):
        rows = pl.ds(k * TILE, TILE)
        image = (ih[rows, :], il[rows, :])
        w = split(weights(image, text, scale, bias))
        image_grad[rows, :] = grad_in[rows, :] + mm(w, text, ROW_COL)
        next_sum[...] = (next_in if k == 0 else next_sum)[...] + mm(w, image, COL_COL)


def last_kernel(scale_ref, bias_ref, piece, th, tl, nh, nl, next_in, back, next_sum, ph, pq, wh, wl):
    piece_body(scale_ref[0], bias_ref[0], piece, th, tl, nh, nl, back, next_sum, ph, pq, wh, wl, next_in)


def rest_kernel(scale_ref, bias_ref, text_in, grad_in, back, *refs):
    text_grad, image_grad = refs[-2:]
    size = back.shape[0]
    image_grad[:size, :] = grad_in[:size, :] + back[...]
    image_grad[size:, :] = grad_in[size:, :]
    total = text_in[...]
    for k in range(0, len(refs) - 2, 4):
        ph, pq, wh, wl = refs[k : k + 4]
        total = total + mm((wh[...], wl[...]), (ph[...], pq[...]), COL_COL)
    text_grad[...] = total


def call(kernel, outs, args, aliases, flops):
    return pl.pallas_call(
        kernel,
        out_shape=[jax.ShapeDtypeStruct(s, d) for s, d in outs],
        in_specs=[SMEM, SMEM] + [VMEM] * (len(args) - 2),
        out_specs=[VMEM] * len(outs),
        input_output_aliases=aliases,
        cost_estimate=pl.CostEstimate(flops=flops, bytes_accessed=2**20, transcendentals=0),
        compiler_params=pltpu.CompilerParams(vmem_limit_bytes=30 * 2**20),
    )(*args)


def shifted(array, axis, by):
    size = lax.axis_size(axis)
    return lax.ppermute(array, axis, [(i, (i + by) % size) for i in range(size)])


def shards(images, texts, partner, scale, bias):
    rows, width = images.shape
    size = rows // 2
    block, half = ((rows, width), F32), ((rows, width), BF16)
    part = [((size, width), F32), block, ((size, width), BF16), ((size, width), BF16)]
    part = part + [((size, rows), BF16), ((size, rows), BF16)]
    work = 6 * rows * rows * width
    text_next = shifted(texts, "inner", -1)
    first = shifted(images[:size], "outer", 1)
    last = shifted(images[size:], "outer", 1)
    image_grad, text_grad, ih, il, th, tl = call(
        own_kernel,
        [block, block, half, half, half, half],
        [scale, bias, images, texts, partner.reshape(rows, 1)],
        {},
        3 * work,
    )
    back0, next_sum, *kept0, nh, nl = call(
        first_kernel, part + [half, half], [scale, bias, first, th, tl, text_next], {}, 3 * work
    )
    back0 = shifted(back0, "outer", -1)
    image_grad, next_sum = call(
        next_kernel, [block, block], [scale, bias, ih, il, nh, nl, image_grad, next_sum], {6: 0, 7: 1}, 3 * work
    )
    back1, next_sum, *kept1 = call(
        last_kernel, part, [scale, bias, last, th, tl, nh, nl, next_sum], {7: 1}, 3 * work
    )
    next_back = shifted(next_sum, "inner", 1)
    back1 = shifted(back1, "outer", -1)
    text_grad, image_grad = call(
        rest_kernel,
        [block, block],
        [scale, bias, text_grad, image_grad, back0, *kept0, *kept1],
        {2: 0, 3: 1},
        REST * work,
    )
    image_grad = image_grad.at[size:].add(back1)
    return image_grad, text_grad + next_back


def solution(mesh):
    placed = (
        P(("outer", "inner"), None),
        P(("outer", "inner"), None),
        P(("outer", "inner"), None),
        P(),
        P(),
    )
    return jax.shard_map(
        shards,
        mesh=mesh,
        in_specs=placed,
        out_specs=(P(("outer", "inner"), None), P(("outer", "inner"), None)),
        check_vma=False,
    )
```

```python
import functools

import jax
import jax.numpy as jnp
from jax import lax
from jax.experimental import pallas as pl
from jax.experimental.pallas import tpu as pltpu
from jax.sharding import PartitionSpec as P

OWN, AHEAD, FIRST, LAST, NEXT, REST_TEXT, REST_IMAGE = 3, 1, 1, 2, 3, 1, 40
TILE = 256
F32, BF16 = jnp.float32, jnp.bfloat16
ROW_ROW = (((1,), (1,)), ((), ()))
ROW_COL = (((1,), (0,)), ((), ()))
COL_COL = (((0,), (0,)), ((), ()))
VMEM = pl.BlockSpec(memory_space=pltpu.VMEM)
SMEM = pl.BlockSpec(memory_space=pltpu.SMEM)
HBM = pl.BlockSpec(memory_space=pltpu.HBM)


def split(x):
    high = x.astype(BF16)
    return high, (x - high.astype(F32)).astype(BF16)


def mm(a, b, dims):
    def one(p, q):
        return lax.dot_general(p, q, dims, preferred_element_type=F32)

    return one(a[0], b[0]) + (one(a[0], b[1]) + one(a[1], b[0]))


def weights(image, text, scale, bias):
    logits = scale * mm(image, text, ROW_ROW) + bias
    return scale * jax.nn.sigmoid(logits)


def split_rows(src, high, low):
    def body(k, carry):
        rows = pl.ds(k * 128, 128)
        high[rows, :], low[rows, :] = split(src[rows, :])
        return carry

    lax.fori_loop(0, src.shape[0] // 128, body, 0)


def store_halves(value, low, high):
    cut = low.shape[0]
    low[...], high[...] = value[:cut], value[cut:]


def own_kernel(scale_ref, bias_ref, images, texts, partner, image_grad, text_grad, ih, il, th, tl):
    scale, bias = scale_ref[0], bias_ref[0]
    split_rows(texts, th, tl)
    split_rows(images, ih, il)
    text = (th[...], tl[...])
    for k in range(images.shape[0] // TILE):
        rows = pl.ds(k * TILE, TILE)
        image = (ih[rows, :], il[rows, :])
        w = weights(image, text, scale, bias)
        columns = lax.broadcasted_iota(jnp.int32, w.shape, 1)
        w = split(w - jnp.where(partner[rows, :] == columns, scale, 0.0))
        image_grad[rows, :] = mm(w, text, ROW_COL)
        term = mm(w, image, COL_COL)
        text_grad[...] = term if k == 0 else text_grad[...] + term


def ahead_kernel(scale_ref, bias_ref, piece, th, tl, ph, pq, wh, wl, total):
    image, text = split(piece[...]), (th[...], tl[...])
    ph[...], pq[...] = image
    w = split(weights(image, text, scale_ref[0], bias_ref[0]))
    wh[...], wl[...] = w
    total[...] = mm(w, text, ROW_COL)


def first_kernel(scale_ref, bias_ref, ph, pq, text_next, total, straight, across, vh, vl, nh, nl):
    split_rows(text_next, nh, nl)
    image, text = (ph[...], pq[...]), (nh[...], nl[...])
    w = split(weights(image, text, scale_ref[0], bias_ref[0]))
    vh[...], vl[...] = w
    store_halves(total[...] + mm(w, text, ROW_COL), straight, across)


def last_kernel(scale_ref, bias_ref, piece, th, tl, nh, nl, straight, across, ph, pq, wh, wl, vh, vl):
    image = split(piece[...])
    ph[...], pq[...] = image
    text = (th[...], tl[...])
    w = split(weights(image, text, scale_ref[0], bias_ref[0]))
    wh[...], wl[...] = w
    total = mm(w, text, ROW_COL)
    text = (nh[...], nl[...])
    w = split(weights(image, text, scale_ref[0], bias_ref[0]))
    vh[...], vl[...] = w
    store_halves(total + mm(w, text, ROW_COL), straight, across)


def next_kernel(scale_ref, bias_ref, ih, il, nh, nl, *refs):
    early, late, uh, ul = refs[-4:]
    text = (nh[...], nl[...])
    for k in range(ih.shape[0] // TILE):
        rows = pl.ds(k * TILE, TILE)
        w = split(weights((ih[rows, :], il[rows, :]), text, scale_ref[0], bias_ref[0]))
        uh[rows, :], ul[rows, :] = w
    total = mm((uh[...], ul[...]), (ih[...], il[...]), COL_COL)
    for ph, pq, vh, vl in (refs[:4], refs[4:8]):
        total = total + mm((vh[...], vl[...]), (ph[...], pq[...]), COL_COL)
    store_halves(total, early, late)


def rest_text_kernel(scale_ref, bias_ref, text_in, *refs):
    total = text_in[...]
    for ph, pq, wh, wl in (refs[:4], refs[4:8]):
        total = total + mm((wh[...], wl[...]), (ph[...], pq[...]), COL_COL)
    store_halves(total, refs[-2], refs[-1])


def rest_image_kernel(scale_ref, bias_ref, grad_in, uh, ul, nh, nl, back0, back1, out, held0, held1, done0, done1, sems):
    cut, size = back0.shape[0], grad_in.shape[0] // 2
    copies = []
    for k, (back, held, done) in enumerate(((back0, held0, done0), (back1, held1, done1))):
        rows = pl.ds(k * size, size)
        total = grad_in[rows, :] + mm((uh[rows, :], ul[rows, :]), (nh[...], nl[...]), ROW_COL)
        done[...] = total[:cut] + back[...]
        copies.append(pltpu.make_async_copy(done, out.at[pl.ds(k * size, cut), :], sems.at[k]))
        copies[-1].start()
        held[...] = total[cut:]
    for copy in copies:
        copy.wait()


def place_kernel(start, held, back, *refs):
    out, buffer, sem = refs[-3:]
    buffer[...] = held[...] + back[...]
    copy = pltpu.make_async_copy(buffer, out.at[pl.ds(start, buffer.shape[0]), :], sem)
    copy.start()
    copy.wait()


def place(held, back, start, out, shape):
    given = [] if out is None else [out]
    return pl.pallas_call(
        functools.partial(place_kernel, start),
        out_shape=jax.ShapeDtypeStruct(shape, F32),
        in_specs=[VMEM, VMEM] + [HBM] * len(given),
        out_specs=HBM,
        scratch_shapes=[pltpu.VMEM(held.shape, F32), pltpu.SemaphoreType.DMA],
        input_output_aliases={2: 0} if given else {},
        compiler_params=pltpu.CompilerParams(vmem_limit_bytes=16 * 2**20),
    )(held, back, *given)


def call(kernel, outs, args, aliases, flops, scratch=(), far=0):
    return pl.pallas_call(
        kernel,
        out_shape=[jax.ShapeDtypeStruct(s, d) for s, d in outs],
        in_specs=[SMEM, SMEM] + [VMEM] * (len(args) - 2),
        out_specs=[HBM] * far + [VMEM] * (len(outs) - far),
        scratch_shapes=list(scratch),
        input_output_aliases=aliases,
        cost_estimate=pl.CostEstimate(flops=flops, bytes_accessed=2**20, transcendentals=0),
        compiler_params=pltpu.CompilerParams(vmem_limit_bytes=30 * 2**20),
    )(*args)


def shifted(array, axis, by):
    size = lax.axis_size(axis)
    return lax.ppermute(array, axis, [(i, (i + by) % size) for i in range(size)])


def crossed(array, at, keep=True):
    half = lax.axis_size("outer") // 2
    pairs = [(i, (i + half) % (2 * half)) for i in range(2 * half) if i % half == at % half]
    if keep:
        pairs += [(i, i) for i in range(2 * half) if i % half != at % half]
    return lax.ppermute(array, "outer", pairs)


def turned(array, by):
    half = lax.axis_size("outer") // 2
    pairs = [(i, i // half * half + (i + by) % half) for i in range(2 * half)]
    return lax.ppermute(array, "outer", pairs)


def tied(*arrays):
    return lax.optimization_barrier(arrays)


def shards(images, texts, partner, scale, bias):
    rows, width = images.shape
    size = rows // 2
    block, half, piece = ((rows, width), F32), ((rows, width), BF16), ((size, width), F32)
    quarter = ((size // 2, width), F32)
    ends = [piece, piece]
    low, w_low = ((size, width), BF16), ((size, rows), BF16)
    work = 6 * rows * rows * width
    last = images[size:]
    last, images, texts = tied(last, images, texts)
    other = crossed(last, -1, False)
    text_next = shifted(texts, "inner", -1)
    first = shifted(images[:size], "outer", 1)
    image_grad, text_grad, ih, il, th, tl = call(
        own_kernel,
        [block, block, half, half, half, half],
        [scale, bias, images, texts, partner.reshape(rows, 1)],
        {},
        OWN * work,
    )
    other, th = tied(other, th)
    outer = lax.axis_size("outer") // 2
    last = jnp.where(lax.axis_index("outer") % outer == outer - 1, other, last)
    last = turned(last, 1)
    *kept0, wh, wl, total = call(
        ahead_kernel, [low, low, w_low, w_low, piece], [scale, bias, first, th, tl], {}, AHEAD * work
    )
    straight0, across0, vh, vl, nh, nl = call(
        first_kernel,
        [quarter, quarter, w_low, w_low, half, half],
        [scale, bias, *kept0, text_next, total],
        {},
        FIRST * work,
    )
    straight0 = shifted(straight0, "outer", -1)
    across0 = crossed(across0, 0)
    mine0, next0 = [*kept0, wh, wl], [*kept0, vh, vl]
    straight1, across1, *kept1 = call(
        last_kernel,
        [quarter, quarter, low, low, w_low, w_low, w_low, w_low],
        [scale, bias, last, th, tl, nh, nl],
        {},
        LAST * work,
    )
    straight1 = shifted(straight1, "outer", -1)
    across1 = crossed(across1, 0)
    mine1, next1 = kept1[:4], kept1[:2] + kept1[4:]
    early, late, uh, ul = call(
        next_kernel,
        [*ends, ((rows, rows), BF16), ((rows, rows), BF16)],
        [scale, bias, ih, il, nh, nl, *next0, *next1],
        {},
        NEXT * work,
    )
    early, late = shifted(early, "inner", 1), shifted(late, "inner", 1)
    uh, text_grad, across0 = tied(uh, text_grad, across0)
    across0 = turned(across0, -1)
    text0, text1 = call(rest_text_kernel, ends, [scale, bias, text_grad, *mine0, *mine1], {}, REST_TEXT * work)
    text0, uh, across1, straight0, straight1 = tied(text0, uh, across1, straight0, straight1)
    across1 = turned(across1, -1)
    image_grad, image0, image1 = call(
        rest_image_kernel,
        [block, quarter, quarter],
        [scale, bias, image_grad, uh, ul, nh, nl, straight0, straight1],
        {},
        REST_IMAGE * work,
        [pltpu.VMEM((size // 2, width), F32)] * 2 + [pltpu.SemaphoreType.DMA((2,))],
        1,
    )
    text_grad = place(text0, early, 0, None, images.shape)
    image_grad = place(image0, across0, size // 2, image_grad, images.shape)
    image_grad = place(image1, across1, size + size // 2, image_grad, images.shape)
    image_grad, late = tied(image_grad, late)
    text_grad = place(text1, late, size, text_grad, images.shape)
    return image_grad, text_grad


def solution(mesh):
    placed = (
        P(("outer", "inner"), None),
        P(("outer", "inner"), None),
        P(("outer", "inner"), None),
        P(),
        P(),
    )
    return jax.shard_map(
        shards,
        mesh=mesh,
        in_specs=placed,
        out_specs=(P(("outer", "inner"), None), P(("outer", "inner"), None)),
        check_vma=False,
    )
```

```python
import functools

import jax
import jax.numpy as jnp
from jax import lax
from jax.experimental import pallas as pl
from jax.experimental.pallas import tpu as pltpu
from jax.sharding import PartitionSpec as P

OWN, AHEAD, FIRST, LAST, NEXT, REST_TEXT, REST_IMAGE = 3, 1, 1, 2, 3, 1, 40
STRAIGHT = 128
TILE = 256
F32, BF16 = jnp.float32, jnp.bfloat16
ROW_ROW = (((1,), (1,)), ((), ()))
ROW_COL = (((1,), (0,)), ((), ()))
COL_COL = (((0,), (0,)), ((), ()))
VMEM = pl.BlockSpec(memory_space=pltpu.VMEM)
SMEM = pl.BlockSpec(memory_space=pltpu.SMEM)
HBM = pl.BlockSpec(memory_space=pltpu.HBM)


def split(x):
    high = x.astype(BF16)
    return high, (x - high.astype(F32)).astype(BF16)


def mm(a, b, dims):
    def one(p, q):
        return lax.dot_general(p, q, dims, preferred_element_type=F32)

    return one(a[0], b[0]) + (one(a[0], b[1]) + one(a[1], b[0]))


def weights(image, text, scale, bias):
    logits = scale * mm(image, text, ROW_ROW) + bias
    return scale * jax.nn.sigmoid(logits)


def split_rows(src, high, low):
    def body(k, carry):
        rows = pl.ds(k * 128, 128)
        high[rows, :], low[rows, :] = split(src[rows, :])
        return carry

    lax.fori_loop(0, src.shape[0] // 128, body, 0)


def store_halves(value, low, high):
    cut = low.shape[0]
    low[...], high[...] = value[:cut], value[cut:]


def split_kernel(scale_ref, bias_ref, images, texts, ih, il, th, tl):
    split_rows(texts, th, tl)
    split_rows(images, ih, il)


def own_kernel(scale_ref, bias_ref, ih, il, th, tl, partner, image_grad, text_grad):
    scale, bias = scale_ref[0], bias_ref[0]
    text = (th[...], tl[...])
    for k in range(ih.shape[0] // TILE):
        rows = pl.ds(k * TILE, TILE)
        image = (ih[rows, :], il[rows, :])
        w = weights(image, text, scale, bias)
        columns = lax.broadcasted_iota(jnp.int32, w.shape, 1)
        w = split(w - jnp.where(partner[rows, :] == columns, scale, 0.0))
        image_grad[rows, :] = mm(w, text, ROW_COL)
        term = mm(w, image, COL_COL)
        text_grad[...] = term if k == 0 else text_grad[...] + term


def ahead_kernel(scale_ref, bias_ref, piece, th, tl, ph, pq, wh, wl, total):
    image, text = split(piece[...]), (th[...], tl[...])
    ph[...], pq[...] = image
    w = split(weights(image, text, scale_ref[0], bias_ref[0]))
    wh[...], wl[...] = w
    total[...] = mm(w, text, ROW_COL)


def first_kernel(scale_ref, bias_ref, ph, pq, text_next, total, straight, across, vh, vl, nh, nl):
    split_rows(text_next, nh, nl)
    image, text = (ph[...], pq[...]), (nh[...], nl[...])
    w = split(weights(image, text, scale_ref[0], bias_ref[0]))
    vh[...], vl[...] = w
    store_halves(total[...] + mm(w, text, ROW_COL), straight, across)


def last_kernel(scale_ref, bias_ref, piece, th, tl, nh, nl, straight, across, ph, pq, wh, wl, vh, vl):
    image = split(piece[...])
    ph[...], pq[...] = image
    text = (th[...], tl[...])
    w = split(weights(image, text, scale_ref[0], bias_ref[0]))
    wh[...], wl[...] = w
    total = mm(w, text, ROW_COL)
    text = (nh[...], nl[...])
    w = split(weights(image, text, scale_ref[0], bias_ref[0]))
    vh[...], vl[...] = w
    store_halves(total + mm(w, text, ROW_COL), straight, across)


def next_kernel(scale_ref, bias_ref, ih, il, nh, nl, *refs):
    early, late, uh, ul = refs[-4:]
    text = (nh[...], nl[...])
    for k in range(ih.shape[0] // TILE):
        rows = pl.ds(k * TILE, TILE)
        w = split(weights((ih[rows, :], il[rows, :]), text, scale_ref[0], bias_ref[0]))
        uh[rows, :], ul[rows, :] = w
    total = mm((uh[...], ul[...]), (ih[...], il[...]), COL_COL)
    for ph, pq, vh, vl in (refs[:4], refs[4:8]):
        total = total + mm((vh[...], vl[...]), (ph[...], pq[...]), COL_COL)
    store_halves(total, early, late)


def rest_text_kernel(scale_ref, bias_ref, text_in, *refs):
    total = text_in[...]
    for ph, pq, wh, wl in (refs[:4], refs[4:8]):
        total = total + mm((wh[...], wl[...]), (ph[...], pq[...]), COL_COL)
    store_halves(total, refs[-2], refs[-1])


def rest_image_kernel(scale_ref, bias_ref, grad_in, uh, ul, nh, nl, back0, out, held0, middle, held1, done, sem):
    cut, size = back0.shape[0], grad_in.shape[0] // 2

    def rows_of(start):
        rows = pl.ds(start, size)
        return grad_in[rows, :] + mm((uh[rows, :], ul[rows, :]), (nh[...], nl[...]), ROW_COL)

    total = rows_of(0)
    done[...] = total[:cut] + back0[...]
    copy = pltpu.make_async_copy(done, out.at[pl.ds(0, cut), :], sem)
    copy.start()
    held0[...] = total[cut:]
    store_halves(rows_of(size), middle, held1)
    copy.wait()


def place_kernel(start, held, back, *refs):
    out, buffer, sem = refs[-3:]
    buffer[...] = held[...] + back[...]
    copy = pltpu.make_async_copy(buffer, out.at[pl.ds(start, buffer.shape[0]), :], sem)
    copy.start()
    copy.wait()


def place(held, back, start, out, shape):
    given = [] if out is None else [out]
    return pl.pallas_call(
        functools.partial(place_kernel, start),
        out_shape=jax.ShapeDtypeStruct(shape, F32),
        in_specs=[VMEM, VMEM] + [HBM] * len(given),
        out_specs=HBM,
        scratch_shapes=[pltpu.VMEM(held.shape, F32), pltpu.SemaphoreType.DMA],
        input_output_aliases={2: 0} if given else {},
        compiler_params=pltpu.CompilerParams(vmem_limit_bytes=16 * 2**20),
    )(held, back, *given)


def call(kernel, outs, args, aliases, flops, scratch=(), far=0):
    return pl.pallas_call(
        kernel,
        out_shape=[jax.ShapeDtypeStruct(s, d) for s, d in outs],
        in_specs=[SMEM, SMEM] + [VMEM] * (len(args) - 2),
        out_specs=[HBM] * far + [VMEM] * (len(outs) - far),
        scratch_shapes=list(scratch),
        input_output_aliases=aliases,
        cost_estimate=pl.CostEstimate(flops=flops, bytes_accessed=2**20, transcendentals=0),
        compiler_params=pltpu.CompilerParams(vmem_limit_bytes=30 * 2**20),
    )(*args)


def shifted(array, axis, by):
    size = lax.axis_size(axis)
    return lax.ppermute(array, axis, [(i, (i + by) % size) for i in range(size)])


def crossed(array, at, keep=True):
    half = lax.axis_size("outer") // 2
    pairs = [(i, (i + half) % (2 * half)) for i in range(2 * half) if i % half == at % half]
    if keep:
        pairs += [(i, i) for i in range(2 * half) if i % half != at % half]
    return lax.ppermute(array, "outer", pairs)


def turned(array, by):
    half = lax.axis_size("outer") // 2
    pairs = [(i, i // half * half + (i + by) % half) for i in range(2 * half)]
    return lax.ppermute(array, "outer", pairs)


def tied(*arrays):
    return lax.optimization_barrier(arrays)


def shards(images, texts, partner, scale, bias):
    rows, width = images.shape
    size = rows // 2
    block, half, piece = ((rows, width), F32), ((rows, width), BF16), ((size, width), F32)
    cut = size * STRAIGHT // 256
    straight, across = ((cut, width), F32), ((size - cut, width), F32)
    ends = [piece, piece]
    low, w_low = ((size, width), BF16), ((size, rows), BF16)
    work = 6 * rows * rows * width
    last = images[size:]
    last, images, texts = tied(last, images, texts)
    other = crossed(last, -1, False)
    text_next = shifted(texts, "inner", -1)
    ih, il, th, tl = call(split_kernel, [half] * 4, [scale, bias, images, texts], {}, 0)
    images, ih = tied(images, ih)
    first = shifted(images[:size], "outer", 1)
    image_grad, text_grad = call(
        own_kernel, [block, block], [scale, bias, ih, il, th, tl, partner.reshape(rows, 1)], {}, OWN * work
    )
    image_grad, th = tied(image_grad, th)
    other, th = tied(other, th)
    outer = lax.axis_size("outer") // 2
    last = jnp.where(lax.axis_index("outer") % outer == outer - 1, other, last)
    last = turned(last, 1)
    *kept0, wh, wl, total = call(
        ahead_kernel, [low, low, w_low, w_low, piece], [scale, bias, first, th, tl], {}, AHEAD * work
    )
    straight0, across0, vh, vl, nh, nl = call(
        first_kernel,
        [straight, across, w_low, w_low, half, half],
        [scale, bias, *kept0, text_next, total],
        {},
        FIRST * work,
    )
    straight0 = shifted(straight0, "outer", -1)
    across0 = crossed(across0, 0)
    mine0, next0 = [*kept0, wh, wl], [*kept0, vh, vl]
    straight1, across1, *kept1 = call(
        last_kernel,
        [straight, across, low, low, w_low, w_low, w_low, w_low],
        [scale, bias, last, th, tl, nh, nl],
        {},
        LAST * work,
    )
    straight1 = shifted(straight1, "outer", -1)
    across1 = crossed(across1, 0)
    mine1, next1 = kept1[:4], kept1[:2] + kept1[4:]
    early, late, uh, ul = call(
        next_kernel,
        [*ends, ((rows, rows), BF16), ((rows, rows), BF16)],
        [scale, bias, ih, il, nh, nl, *next0, *next1],
        {},
        NEXT * work,
    )
    early, late = shifted(early, "inner", 1), shifted(late, "inner", 1)
    uh, text_grad, across0, straight0 = tied(uh, text_grad, across0, straight0)
    across0 = turned(across0, -1)
    text0, text1 = call(rest_text_kernel, ends, [scale, bias, text_grad, *mine0, *mine1], {}, REST_TEXT * work)
    text0, uh, across1 = tied(text0, uh, across1)
    across1 = turned(across1, -1)
    image_grad, image0, middle, image1 = call(
        rest_image_kernel,
        [block, across, straight, across],
        [scale, bias, image_grad, uh, ul, nh, nl, straight0],
        {},
        REST_IMAGE * work,
        [pltpu.VMEM((cut, width), F32), pltpu.SemaphoreType.DMA],
        1,
    )
    image_grad = place(middle, straight1, size, image_grad, images.shape)
    image_grad = place(image0, across0, cut, image_grad, images.shape)
    text_grad = place(text0, early, 0, None, images.shape)
    image_grad, text_grad = tied(image_grad, text_grad)
    image_grad = place(image1, across1, size + cut, image_grad, images.shape)
    image_grad, late = tied(image_grad, late)
    text_grad = place(text1, late, size, text_grad, images.shape)
    return image_grad, text_grad


def solution(mesh):
    placed = (
        P(("outer", "inner"), None),
        P(("outer", "inner"), None),
        P(("outer", "inner"), None),
        P(),
        P(),
    )
    return jax.shard_map(
        shards,
        mesh=mesh,
        in_specs=placed,
        out_specs=(P(("outer", "inner"), None), P(("outer", "inner"), None)),
        check_vma=False,
    )
```

```python
import functools

import jax
import jax.numpy as jnp
from jax import lax
from jax.experimental import pallas as pl
from jax.experimental.pallas import tpu as pltpu
from jax.sharding import PartitionSpec as P

OWN, AHEAD, FIRST, LAST, NEXT, REST_TEXT, REST_IMAGE = 3, 1, 1, 2, 3, 1, 40
STRAIGHT = 128
TILE = 256
F32, BF16 = jnp.float32, jnp.bfloat16
ROW_ROW = (((1,), (1,)), ((), ()))
ROW_COL = (((1,), (0,)), ((), ()))
COL_COL = (((0,), (0,)), ((), ()))
VMEM = pl.BlockSpec(memory_space=pltpu.VMEM)
SMEM = pl.BlockSpec(memory_space=pltpu.SMEM)
HBM = pl.BlockSpec(memory_space=pltpu.HBM)


def split(x):
    high = x.astype(BF16)
    return high, (x - high.astype(F32)).astype(BF16)


def mm(a, b, dims):
    def one(p, q):
        return lax.dot_general(p, q, dims, preferred_element_type=F32)

    return one(a[0], b[0]) + (one(a[0], b[1]) + one(a[1], b[0]))


def weights(image, text, scale, bias):
    logits = scale * mm(image, text, ROW_ROW) + bias
    return scale * jax.nn.sigmoid(logits)


def split_rows(src, high, low):
    def body(k, carry):
        rows = pl.ds(k * 128, 128)
        high[rows, :], low[rows, :] = split(src[rows, :])
        return carry

    lax.fori_loop(0, src.shape[0] // 128, body, 0)


def store_halves(value, low, high):
    cut = low.shape[0]
    low[...], high[...] = value[:cut], value[cut:]


def split_kernel(scale_ref, bias_ref, images, texts, ih, il, th, tl):
    split_rows(texts, th, tl)
    split_rows(images, ih, il)


def own_kernel(scale_ref, bias_ref, ih, il, th, tl, partner, image_grad, text_grad):
    scale, bias = scale_ref[0], bias_ref[0]
    text = (th[...], tl[...])
    for k in range(ih.shape[0] // TILE):
        rows = pl.ds(k * TILE, TILE)
        image = (ih[rows, :], il[rows, :])
        w = weights(image, text, scale, bias)
        columns = lax.broadcasted_iota(jnp.int32, w.shape, 1)
        w = split(w - jnp.where(partner[rows, :] == columns, scale, 0.0))
        image_grad[rows, :] = mm(w, text, ROW_COL)
        term = mm(w, image, COL_COL)
        text_grad[...] = term if k == 0 else text_grad[...] + term


def ahead_kernel(scale_ref, bias_ref, piece, th, tl, ph, pq, wh, wl, total):
    image, text = split(piece[...]), (th[...], tl[...])
    ph[...], pq[...] = image
    w = split(weights(image, text, scale_ref[0], bias_ref[0]))
    wh[...], wl[...] = w
    total[...] = mm(w, text, ROW_COL)


def first_kernel(scale_ref, bias_ref, ph, pq, text_next, total, straight, across, vh, vl, nh, nl):
    split_rows(text_next, nh, nl)
    image, text = (ph[...], pq[...]), (nh[...], nl[...])
    w = split(weights(image, text, scale_ref[0], bias_ref[0]))
    vh[...], vl[...] = w
    store_halves(total[...] + mm(w, text, ROW_COL), straight, across)


def last_kernel(scale_ref, bias_ref, piece, th, tl, nh, nl, straight, across, ph, pq, wh, wl, vh, vl):
    image = split(piece[...])
    ph[...], pq[...] = image
    text = (th[...], tl[...])
    w = split(weights(image, text, scale_ref[0], bias_ref[0]))
    wh[...], wl[...] = w
    total = mm(w, text, ROW_COL)
    text = (nh[...], nl[...])
    w = split(weights(image, text, scale_ref[0], bias_ref[0]))
    vh[...], vl[...] = w
    store_halves(total + mm(w, text, ROW_COL), straight, across)


def next_kernel(scale_ref, bias_ref, ih, il, nh, nl, *refs):
    early, late, uh, ul = refs[-4:]
    text = (nh[...], nl[...])
    for k in range(ih.shape[0] // TILE):
        rows = pl.ds(k * TILE, TILE)
        w = split(weights((ih[rows, :], il[rows, :]), text, scale_ref[0], bias_ref[0]))
        uh[rows, :], ul[rows, :] = w
    total = mm((uh[...], ul[...]), (ih[...], il[...]), COL_COL)
    for ph, pq, vh, vl in (refs[:4], refs[4:8]):
        total = total + mm((vh[...], vl[...]), (ph[...], pq[...]), COL_COL)
    store_halves(total, early, late)


def rest_text_kernel(scale_ref, bias_ref, text_in, *refs):
    total = text_in[...]
    for ph, pq, wh, wl in (refs[:4], refs[4:8]):
        total = total + mm((wh[...], wl[...]), (ph[...], pq[...]), COL_COL)
    store_halves(total, refs[-2], refs[-1])


def rest_image_kernel(scale_ref, bias_ref, grad_in, uh, ul, nh, nl, back0, out, held0, middle, held1, done, sem):
    cut, size = back0.shape[0], grad_in.shape[0] // 2

    def rows_of(start):
        rows = pl.ds(start, size)
        return grad_in[rows, :] + mm((uh[rows, :], ul[rows, :]), (nh[...], nl[...]), ROW_COL)

    total = rows_of(0)
    done[...] = total[:cut] + back0[...]
    copy = pltpu.make_async_copy(done, out.at[pl.ds(0, cut), :], sem)
    copy.start()
    held0[...] = total[cut:]
    store_halves(rows_of(size), middle, held1)
    copy.wait()


def place_kernel(start, held, back, *refs):
    out, buffer, sem = refs[-3:]
    buffer[...] = held[...] + back[...]
    copy = pltpu.make_async_copy(buffer, out.at[pl.ds(start, buffer.shape[0]), :], sem)
    copy.start()
    copy.wait()


def place(held, back, start, out, shape):
    given = [] if out is None else [out]
    return pl.pallas_call(
        functools.partial(place_kernel, start),
        out_shape=jax.ShapeDtypeStruct(shape, F32),
        in_specs=[VMEM, VMEM] + [HBM] * len(given),
        out_specs=HBM,
        scratch_shapes=[pltpu.VMEM(held.shape, F32), pltpu.SemaphoreType.DMA],
        input_output_aliases={2: 0} if given else {},
        compiler_params=pltpu.CompilerParams(vmem_limit_bytes=16 * 2**20),
    )(held, back, *given)


def call(kernel, outs, args, aliases, flops, scratch=(), far=0):
    return pl.pallas_call(
        kernel,
        out_shape=[jax.ShapeDtypeStruct(s, d) for s, d in outs],
        in_specs=[SMEM, SMEM] + [VMEM] * (len(args) - 2),
        out_specs=[HBM] * far + [VMEM] * (len(outs) - far),
        scratch_shapes=list(scratch),
        input_output_aliases=aliases,
        cost_estimate=pl.CostEstimate(flops=flops, bytes_accessed=2**20, transcendentals=0),
        compiler_params=pltpu.CompilerParams(vmem_limit_bytes=30 * 2**20),
    )(*args)


def shifted(array, axis, by):
    size = lax.axis_size(axis)
    return lax.ppermute(array, axis, [(i, (i + by) % size) for i in range(size)])


def crossed(array, at):
    half = lax.axis_size("outer") // 2
    pairs = [(i, (i + half) % (2 * half) if i % half == at % half else i) for i in range(2 * half)]
    return lax.ppermute(array, "outer", pairs)


def exchanged(array):
    half, inner = lax.axis_size("outer") // 2, lax.axis_size("inner")
    ends = ((half - 1, 2 * half - 1), (2 * half - 1, half - 1))
    pairs = [(a * inner + i, b * inner + i) for a, b in ends for i in range(0, inner, 2)]
    return lax.ppermute(array, ("outer", "inner"), pairs)


def advanced(array):
    half, inner = lax.axis_size("outer") // 2, lax.axis_size("inner")
    pairs = []
    for o in range(2 * half):
        for i in range(inner):
            to = (o + 1) % (2 * half) if i % 2 else o // half * half + (o + 1) % half
            pairs.append((o * inner + i, to * inner + i))
    return lax.ppermute(array, ("outer", "inner"), pairs)


def turned(array, by):
    half = lax.axis_size("outer") // 2
    pairs = [(i, i // half * half + (i + by) % half) for i in range(2 * half)]
    return lax.ppermute(array, "outer", pairs)


def tied(*arrays):
    return lax.optimization_barrier(arrays)


def shards(images, texts, partner, scale, bias):
    rows, width = images.shape
    size = rows // 2
    block, half, piece = ((rows, width), F32), ((rows, width), BF16), ((size, width), F32)
    cut = size * STRAIGHT // 256
    straight, across = ((cut, width), F32), ((size - cut, width), F32)
    ends = [piece, piece]
    low, w_low = ((size, width), BF16), ((size, rows), BF16)
    work = 6 * rows * rows * width
    text_next = shifted(texts, "inner", -1)
    other = exchanged(images)
    ih, il, th, tl = call(split_kernel, [half] * 4, [scale, bias, images, texts], {}, 0)
    other, images, ih = tied(other, images, ih)
    half_outer = lax.axis_size("outer") // 2
    edge = lax.axis_index("outer") % half_outer == half_outer - 1
    take = jnp.logical_and(edge, lax.axis_index("inner") % 2 == 0)
    first = jnp.where(take, other[:size], images[:size])
    first, images, other = tied(first, images, other)
    last = jnp.where(take, other[size:], images[size:])
    last, ih = tied(last, ih)
    first, last = advanced(first), advanced(last)
    image_grad, text_grad = call(
        own_kernel, [block, block], [scale, bias, ih, il, th, tl, partner.reshape(rows, 1)], {}, OWN * work
    )
    image_grad, th = tied(image_grad, th)
    *kept0, wh, wl, total = call(
        ahead_kernel, [low, low, w_low, w_low, piece], [scale, bias, first, th, tl], {}, AHEAD * work
    )
    straight0, across0, vh, vl, nh, nl = call(
        first_kernel,
        [straight, across, w_low, w_low, half, half],
        [scale, bias, *kept0, text_next, total],
        {},
        FIRST * work,
    )
    straight0 = shifted(straight0, "outer", -1)
    across0 = crossed(across0, 0)
    mine0, next0 = [*kept0, wh, wl], [*kept0, vh, vl]
    straight1, across1, *kept1 = call(
        last_kernel,
        [straight, across, low, low, w_low, w_low, w_low, w_low],
        [scale, bias, last, th, tl, nh, nl],
        {},
        LAST * work,
    )
    straight1 = shifted(straight1, "outer", -1)
    across1 = crossed(across1, 0)
    mine1, next1 = kept1[:4], kept1[:2] + kept1[4:]
    early, late, uh, ul = call(
        next_kernel,
        [*ends, ((rows, rows), BF16), ((rows, rows), BF16)],
        [scale, bias, ih, il, nh, nl, *next0, *next1],
        {},
        NEXT * work,
    )
    early, late = shifted(early, "inner", 1), shifted(late, "inner", 1)
    uh, text_grad, across0, straight0 = tied(uh, text_grad, across0, straight0)
    across0 = turned(across0, -1)
    text0, text1 = call(rest_text_kernel, ends, [scale, bias, text_grad, *mine0, *mine1], {}, REST_TEXT * work)
    text0, uh, across1 = tied(text0, uh, across1)
    across1 = turned(across1, -1)
    image_grad, image0, middle, image1 = call(
        rest_image_kernel,
        [block, across, straight, across],
        [scale, bias, image_grad, uh, ul, nh, nl, straight0],
        {},
        REST_IMAGE * work,
        [pltpu.VMEM((cut, width), F32), pltpu.SemaphoreType.DMA],
        1,
    )
    image_grad = place(middle, straight1, size, image_grad, images.shape)
    image_grad = place(image0, across0, cut, image_grad, images.shape)
    text_grad = place(text0, early, 0, None, images.shape)
    image_grad, text_grad = tied(image_grad, text_grad)
    image_grad = place(image1, across1, size + cut, image_grad, images.shape)
    image_grad, late = tied(image_grad, late)
    text_grad = place(text1, late, size, text_grad, images.shape)
    return image_grad, text_grad


def solution(mesh):
    placed = (
        P(("outer", "inner"), None),
        P(("outer", "inner"), None),
        P(("outer", "inner"), None),
        P(),
        P(),
    )
    return jax.shard_map(
        shards,
        mesh=mesh,
        in_specs=placed,
        out_specs=(P(("outer", "inner"), None), P(("outer", "inner"), None)),
        check_vma=False,
    )
```

```python
import functools

import jax
import jax.numpy as jnp
from jax import lax
from jax.experimental import pallas as pl
from jax.experimental.pallas import tpu as pltpu
from jax.sharding import PartitionSpec as P

OWN, AHEAD, FIRST, LAST, NEXT, REST_TEXT, REST_IMAGE = 3, 1, 1, 2, 3, 1, 40
STRAIGHT = 128
TILE = 256
F32, BF16 = jnp.float32, jnp.bfloat16
ROW_ROW = (((1,), (1,)), ((), ()))
ROW_COL = (((1,), (0,)), ((), ()))
COL_COL = (((0,), (0,)), ((), ()))
VMEM = pl.BlockSpec(memory_space=pltpu.VMEM)
SMEM = pl.BlockSpec(memory_space=pltpu.SMEM)
HBM = pl.BlockSpec(memory_space=pltpu.HBM)


def split(x):
    high = x.astype(BF16)
    return high, (x - high.astype(F32)).astype(BF16)


def mm(a, b, dims):
    def one(p, q):
        return lax.dot_general(p, q, dims, preferred_element_type=F32)

    return one(a[0], b[0]) + (one(a[0], b[1]) + one(a[1], b[0]))


def weights(image, text, scale, bias):
    logits = scale * mm(image, text, ROW_ROW) + bias
    return scale * jax.nn.sigmoid(logits)


def split_rows(src, high, low):
    def body(k, carry):
        rows = pl.ds(k * 128, 128)
        high[rows, :], low[rows, :] = split(src[rows, :])
        return carry

    lax.fori_loop(0, src.shape[0] // 128, body, 0)


def store_halves(value, low, high):
    cut = low.shape[0]
    low[...], high[...] = value[:cut], value[cut:]


def split_kernel(scale_ref, bias_ref, images, texts, ih, il, th, tl):
    split_rows(texts, th, tl)
    split_rows(images, ih, il)


def own_kernel(scale_ref, bias_ref, ih, il, th, tl, partner, image_grad, text_grad):
    scale, bias = scale_ref[0], bias_ref[0]
    text = (th[...], tl[...])
    for k in range(ih.shape[0] // TILE):
        rows = pl.ds(k * TILE, TILE)
        image = (ih[rows, :], il[rows, :])
        w = weights(image, text, scale, bias)
        columns = lax.broadcasted_iota(jnp.int32, w.shape, 1)
        w = split(w - jnp.where(partner[rows, :] == columns, scale, 0.0))
        image_grad[rows, :] = mm(w, text, ROW_COL)
        term = mm(w, image, COL_COL)
        text_grad[...] = term if k == 0 else text_grad[...] + term


def ahead_kernel(scale_ref, bias_ref, piece, th, tl, ph, pq, wh, wl, total):
    image, text = split(piece[...]), (th[...], tl[...])
    ph[...], pq[...] = image
    w = split(weights(image, text, scale_ref[0], bias_ref[0]))
    wh[...], wl[...] = w
    total[...] = mm(w, text, ROW_COL)


def first_kernel(scale_ref, bias_ref, ph, pq, text_next, total, straight, across, vh, vl, nh, nl):
    split_rows(text_next, nh, nl)
    image, text = (ph[...], pq[...]), (nh[...], nl[...])
    w = split(weights(image, text, scale_ref[0], bias_ref[0]))
    vh[...], vl[...] = w
    store_halves(total[...] + mm(w, text, ROW_COL), straight, across)


def last_kernel(scale_ref, bias_ref, piece, th, tl, nh, nl, straight, across, ph, pq, wh, wl, vh, vl):
    image = split(piece[...])
    ph[...], pq[...] = image
    text = (th[...], tl[...])
    w = split(weights(image, text, scale_ref[0], bias_ref[0]))
    wh[...], wl[...] = w
    total = mm(w, text, ROW_COL)
    text = (nh[...], nl[...])
    w = split(weights(image, text, scale_ref[0], bias_ref[0]))
    vh[...], vl[...] = w
    store_halves(total + mm(w, text, ROW_COL), straight, across)


def next_kernel(scale_ref, bias_ref, ih, il, nh, nl, *refs):
    early, late, uh, ul = refs[-4:]
    text = (nh[...], nl[...])
    for k in range(ih.shape[0] // TILE):
        rows = pl.ds(k * TILE, TILE)
        w = split(weights((ih[rows, :], il[rows, :]), text, scale_ref[0], bias_ref[0]))
        uh[rows, :], ul[rows, :] = w
    total = mm((uh[...], ul[...]), (ih[...], il[...]), COL_COL)
    for ph, pq, vh, vl in (refs[:4], refs[4:8]):
        total = total + mm((vh[...], vl[...]), (ph[...], pq[...]), COL_COL)
    store_halves(total, early, late)


def rest_text_kernel(scale_ref, bias_ref, text_in, *refs):
    total = text_in[...]
    for ph, pq, wh, wl in (refs[:4], refs[4:8]):
        total = total + mm((wh[...], wl[...]), (ph[...], pq[...]), COL_COL)
    store_halves(total, refs[-2], refs[-1])


def rest_image_kernel(scale_ref, bias_ref, grad_in, uh, ul, nh, nl, back0, out, held0, middle, held1, done, sem):
    cut, size = back0.shape[0], grad_in.shape[0] // 2

    def rows_of(start):
        rows = pl.ds(start, size)
        return grad_in[rows, :] + mm((uh[rows, :], ul[rows, :]), (nh[...], nl[...]), ROW_COL)

    total = rows_of(0)
    done[...] = total[:cut] + back0[...]
    copy = pltpu.make_async_copy(done, out.at[pl.ds(0, cut), :], sem)
    copy.start()
    held0[...] = total[cut:]
    store_halves(rows_of(size), middle, held1)
    copy.wait()


def place_kernel(start, held, back, *refs):
    out, buffer, sem = refs[-3:]
    buffer[...] = held[...] + back[...]
    copy = pltpu.make_async_copy(buffer, out.at[pl.ds(start, buffer.shape[0]), :], sem)
    copy.start()
    copy.wait()


def place(held, back, start, out, shape):
    given = [] if out is None else [out]
    return pl.pallas_call(
        functools.partial(place_kernel, start),
        out_shape=jax.ShapeDtypeStruct(shape, F32),
        in_specs=[VMEM, VMEM] + [HBM] * len(given),
        out_specs=HBM,
        scratch_shapes=[pltpu.VMEM(held.shape, F32), pltpu.SemaphoreType.DMA],
        input_output_aliases={2: 0} if given else {},
        compiler_params=pltpu.CompilerParams(vmem_limit_bytes=16 * 2**20),
    )(held, back, *given)


def call(kernel, outs, args, aliases, flops, scratch=(), far=0):
    return pl.pallas_call(
        kernel,
        out_shape=[jax.ShapeDtypeStruct(s, d) for s, d in outs],
        in_specs=[SMEM, SMEM] + [VMEM] * (len(args) - 2),
        out_specs=[HBM] * far + [VMEM] * (len(outs) - far),
        scratch_shapes=list(scratch),
        input_output_aliases=aliases,
        cost_estimate=pl.CostEstimate(flops=flops, bytes_accessed=2**20, transcendentals=0),
        compiler_params=pltpu.CompilerParams(vmem_limit_bytes=30 * 2**20),
    )(*args)


def shifted(array, axis, by):
    size = lax.axis_size(axis)
    return lax.ppermute(array, axis, [(i, (i + by) % size) for i in range(size)])


def crossed(array, at):
    half = lax.axis_size("outer") // 2
    pairs = [(i, (i + half) % (2 * half) if i % half == at % half else i) for i in range(2 * half)]
    return lax.ppermute(array, "outer", pairs)


def exchanged(array):
    half, inner = lax.axis_size("outer") // 2, lax.axis_size("inner")
    ends = ((half - 1, 2 * half - 1), (2 * half - 1, half - 1))
    pairs = [(a * inner + i, b * inner + i) for a, b in ends for i in range(0, inner, 2)]
    return lax.ppermute(array, ("outer", "inner"), pairs)


def advanced(array):
    half, inner = lax.axis_size("outer") // 2, lax.axis_size("inner")
    pairs = []
    for o in range(2 * half):
        for i in range(inner):
            to = (o + 1) % (2 * half) if i % 2 else o // half * half + (o + 1) % half
            pairs.append((o * inner + i, to * inner + i))
    return lax.ppermute(array, ("outer", "inner"), pairs)


def turned(array, by):
    half = lax.axis_size("outer") // 2
    pairs = [(i, i // half * half + (i + by) % half) for i in range(2 * half)]
    return lax.ppermute(array, "outer", pairs)


def tied(*arrays):
    return lax.optimization_barrier(arrays)


def shards(images, texts, partner, scale, bias):
    rows, width = images.shape
    size = rows // 2
    block, half, piece = ((rows, width), F32), ((rows, width), BF16), ((size, width), F32)
    cut = size * STRAIGHT // 256
    straight, across = ((cut, width), F32), ((size - cut, width), F32)
    ends = [piece, piece]
    low, w_low = ((size, width), BF16), ((size, rows), BF16)
    work = 6 * rows * rows * width
    text_next = shifted(texts, "inner", -1)
    other = exchanged(images)
    half_outer = lax.axis_size("outer") // 2
    edge = lax.axis_index("outer") % half_outer == half_outer - 1
    take = jnp.logical_and(edge, lax.axis_index("inner") % 2 == 0)
    first = jnp.where(take, other[:size], images[:size])
    first, images, other, texts = tied(first, images, other, texts)
    ih, il, th, tl = call(split_kernel, [half] * 4, [scale, bias, images, texts], {}, 0)
    last = jnp.where(take, other[size:], images[size:])
    last, ih = tied(last, ih)
    first, last = advanced(first), advanced(last)
    image_grad, text_grad = call(
        own_kernel, [block, block], [scale, bias, ih, il, th, tl, partner.reshape(rows, 1)], {}, OWN * work
    )
    image_grad, th = tied(image_grad, th)
    *kept0, wh, wl, total = call(
        ahead_kernel, [low, low, w_low, w_low, piece], [scale, bias, first, th, tl], {}, AHEAD * work
    )
    straight0, across0, vh, vl, nh, nl = call(
        first_kernel,
        [straight, across, w_low, w_low, half, half],
        [scale, bias, *kept0, text_next, total],
        {},
        FIRST * work,
    )
    straight0 = shifted(straight0, "outer", -1)
    across0 = crossed(across0, 0)
    mine0, next0 = [*kept0, wh, wl], [*kept0, vh, vl]
    straight1, across1, *kept1 = call(
        last_kernel,
        [straight, across, low, low, w_low, w_low, w_low, w_low],
        [scale, bias, last, th, tl, nh, nl],
        {},
        LAST * work,
    )
    straight1 = shifted(straight1, "outer", -1)
    across1 = crossed(across1, 0)
    mine1, next1 = kept1[:4], kept1[:2] + kept1[4:]
    early, late, uh, ul = call(
        next_kernel,
        [*ends, ((rows, rows), BF16), ((rows, rows), BF16)],
        [scale, bias, ih, il, nh, nl, *next0, *next1],
        {},
        NEXT * work,
    )
    early, late = shifted(early, "inner", 1), shifted(late, "inner", 1)
    uh, text_grad, across0, straight0 = tied(uh, text_grad, across0, straight0)
    across0 = turned(across0, -1)
    text0, text1 = call(rest_text_kernel, ends, [scale, bias, text_grad, *mine0, *mine1], {}, REST_TEXT * work)
    text0, uh, across1 = tied(text0, uh, across1)
    across1 = turned(across1, -1)
    image_grad, image0, middle, image1 = call(
        rest_image_kernel,
        [block, across, straight, across],
        [scale, bias, image_grad, uh, ul, nh, nl, straight0],
        {},
        REST_IMAGE * work,
        [pltpu.VMEM((cut, width), F32), pltpu.SemaphoreType.DMA],
        1,
    )
    image_grad = place(middle, straight1, size, image_grad, images.shape)
    image_grad = place(image0, across0, cut, image_grad, images.shape)
    text_grad = place(text0, early, 0, None, images.shape)
    image_grad, text_grad = tied(image_grad, text_grad)
    image_grad = place(image1, across1, size + cut, image_grad, images.shape)
    image_grad, late = tied(image_grad, late)
    text_grad = place(text1, late, size, text_grad, images.shape)
    return image_grad, text_grad


def solution(mesh):
    placed = (
        P(("outer", "inner"), None),
        P(("outer", "inner"), None),
        P(("outer", "inner"), None),
        P(),
        P(),
    )
    return jax.shard_map(
        shards,
        mesh=mesh,
        in_specs=placed,
        out_specs=(P(("outer", "inner"), None), P(("outer", "inner"), None)),
        check_vma=False,
    )
```
